32 devices in a mesh: ctx: 4 (over x, core), fsdp: 8 (over z, y).
Axes of the slice: x: 2, y: 2, z: 4, core: 2. Of those that a mesh axis runs over, the one named last changes fastest.
Arguments:
- query: bfloat16 [2, 8192, 4096], P(None, ('ctx', 'fsdp')), may hold values from -64 to 64
- key: bfloat16 [2, 8192, 2048], P(None, ('ctx', 'fsdp')), may hold values from -32 to 32
- value: bfloat16 [2, 8192, 2048], P(None, ('ctx', 'fsdp')), may hold values from -6 to 6
- grad_out: bfloat16 [2, 8192, 4096], P(None, ('ctx', 'fsdp')), may hold values from -6 to 6
- tile_start: int32 [2, 64], replicated, may hold values from 0 to 63, as said below
Outputs:
- grad_query: bfloat16 [2, 8192, 4096], P(None, ('ctx', 'fsdp'))
- grad_key: bfloat16 [2, 8192, 2048], P(None, ('ctx', 'fsdp'))
- grad_value: bfloat16 [2, 8192, 2048], P(None, ('ctx', 'fsdp'))
The draws below stay inside these ranges and needn't reach their ends.
Inputs may be any that keep to these rules, and one draw needn't show every extreme that they name: tile_start[b, t] is the first tile of the document holding tile t: it equals t or tile_start[b, t - 1], and tile_start[b, 0] = 0; the last tile of every sequence begins a document; no document begins at a tile whose first token is a nonzero multiple of 2048.
All inputs are finite; a program needn't handle non-finite values.
Results may differ from the reference program's by a relative error of at most 0.012.
Values may be sent and summed in bfloat16 or wider, within the bound.
No kernel may reach another device: no remote copies, remote signals or barrier semaphores. Data moves between devices by JAX's collectives and lax.ppermute only.
A program may use at most 192 MiB of HBM per device.

```python
import jax
import jax.numpy as jnp
from jax import lax

HEADS = 32
KV_HEADS = 16
HEAD_DIM = 128
WINDOW = 1024
SEQ_LEN = 8192
TILE = 128
QBLOCK = 512
SEQS = 2
BLOCK_LEN = 2048


def shared_keys(key):
    shape = (SEQS, SEQ_LEN, KV_HEADS, HEAD_DIM)
    base = jnp.clip(jax.random.normal(jax.random.fold_in(key, 101), shape, jnp.float32), -6.0, 6.0)
    return base


def draw_key(key, part):
    return shared_keys(key).reshape(SEQS, SEQ_LEN, KV_HEADS * HEAD_DIM).astype(jnp.bfloat16)


def draw_query(key, part):
    shape = (SEQS, SEQ_LEN, HEADS, HEAD_DIM)
    base = jnp.clip(jax.random.normal(jax.random.fold_in(key, 201), shape, jnp.float32), -6.0, 6.0)
    return base.reshape(SEQS, SEQ_LEN, HEADS * HEAD_DIM).astype(jnp.bfloat16)


def draw_tile_start(key, part):
    tiles = SEQ_LEN // TILE
    levels = jax.random.randint(jax.random.fold_in(key, 301), (SEQS, 8), 0, 4)
    table = jnp.array([0, 1, 4, 12], jnp.int32)
    limits = jnp.sum(jnp.where(levels[:, :, None] == jnp.arange(4)[None, None, :], table[None, None, :], 0), axis=2)
    limits = jnp.repeat(limits, tiles // 8, axis=1)
    rolls = jax.random.randint(jax.random.fold_in(key, 302), (SEQS, tiles), 0, 16)
    place = jnp.arange(tiles, dtype=jnp.int32)[None, :]
    begins = (rolls < limits) & (place % (BLOCK_LEN // TILE) != 0)
    begins = begins | (place == 0) | (place == tiles - 1)
    marks = jnp.where(begins, place, 0).astype(jnp.int32)
    return lax.cummax(marks, axis=1)


def level_of(key, extent, shards, low, largest):
    gain = 1.0
    for position, blocks in shards:
        draws = jax.random.uniform(jax.random.fold_in(jax.random.fold_in(key, 6), position), (blocks,), jnp.float32, low / len(shards), largest / len(shards))
        gain = gain * jnp.repeat(jnp.exp(draws), extent[position] // blocks).reshape((-1,) + (1,) * (len(extent) - 1 - position))
    return gain


def noise(stream_key, extent, width, most, split=(), held_as=jnp.bfloat16):
    values = jax.random.normal(stream_key, extent, jnp.float32) * width
    if len(split) > 0:
        values = level_of(stream_key, extent, split, -0.22, 0.18) * values
    return jnp.clip(values, min=-most, max=most).astype(held_as)


def setup_inputs(seed: int = 0) -> dict:
    key_of = jax.random.split(jax.random.key(seed), 6)
    query = draw_query(jax.random.fold_in(key_of[5], 71), 0)
    key = draw_key(jax.random.fold_in(key_of[5], 71), 0)
    value = noise(key_of[2], (SEQS, SEQ_LEN, KV_HEADS * HEAD_DIM), 1.0, 6.0, ((1, 32),))
    grad_out = noise(key_of[3], (SEQS, SEQ_LEN, HEADS * HEAD_DIM), 1.0, 6.0, ((1, 32),))
    tile_start = draw_tile_start(jax.random.fold_in(key_of[5], 71), 0)
    return {"query": query, "key": key, "value": value, "grad_out": grad_out, "tile_start": tile_start}


score_scale = 168.0 ** -0.5


def block_grads(q_blk, g_blk, k_span, v_span, visible):
    hi = lax.Precision.HIGHEST
    qf = q_blk.astype(jnp.float32)
    gf = g_blk.astype(jnp.float32)
    kf = k_span.astype(jnp.float32)
    vf = v_span.astype(jnp.float32)
    scores = jnp.einsum("qhd,khd->hqk", qf, kf, precision=hi) * score_scale
    top = jnp.max(jnp.where(visible, scores, -jnp.inf), axis=-1, keepdims=True)
    weights = jnp.exp(jnp.where(visible, scores - top, -jnp.inf))
    probs = weights / jnp.sum(weights, axis=-1, keepdims=True)
    probs_low = probs.astype(jnp.bfloat16)
    grad_probs = jnp.einsum("qhd,khd->hqk", gf, vf, precision=hi)
    delta = jnp.sum(probs * grad_probs, axis=-1, keepdims=True)
    grad_scores = (probs * (grad_probs - delta)).astype(jnp.bfloat16)
    gsf = grad_scores.astype(jnp.float32)
    grad_q = (jnp.einsum("hqk,khd->qhd", gsf, kf, precision=hi) * score_scale).astype(jnp.bfloat16)
    grad_k = jnp.einsum("hqk,qhd->khd", gsf, qf, precision=hi) * score_scale
    grad_v = jnp.einsum("hqk,qhd->khd", probs_low.astype(jnp.float32), gf, precision=hi)
    return grad_q, grad_k, grad_v


def one_sequence(query, key, value, grad_out, tiles):
    span = QBLOCK + WINDOW
    q_all = query.reshape(SEQ_LEN, HEADS, HEAD_DIM)
    g_all = grad_out.reshape(SEQ_LEN, HEADS, HEAD_DIM)
    k_all = jnp.repeat(key.reshape(SEQ_LEN, KV_HEADS, HEAD_DIM), 2, axis=1)
    v_all = jnp.repeat(value.reshape(SEQ_LEN, KV_HEADS, HEAD_DIM), 2, axis=1)
    padding = jnp.zeros((WINDOW, HEADS, HEAD_DIM), k_all.dtype)
    k_ext = jnp.concatenate([padding, k_all], axis=0)
    v_ext = jnp.concatenate([padding, v_all], axis=0)
    starts = TILE * jnp.repeat(tiles, TILE)

    def step(index, carry):
        grad_q, grad_k, grad_v = carry
        q0 = jnp.asarray(index, jnp.int32) * QBLOCK
        q_blk = lax.dynamic_slice_in_dim(q_all, q0, QBLOCK, 0)
        g_blk = lax.dynamic_slice_in_dim(g_all, q0, QBLOCK, 0)
        k_span = lax.dynamic_slice_in_dim(k_ext, q0, span, 0)
        v_span = lax.dynamic_slice_in_dim(v_ext, q0, span, 0)
        qpos = q0 + jnp.arange(QBLOCK, dtype=jnp.int32)
        kpos = q0 - WINDOW + jnp.arange(span, dtype=jnp.int32)
        first = lax.dynamic_slice_in_dim(starts, q0, QBLOCK, 0)
        visible = (kpos[None, :] >= first[:, None]) & (kpos[None, :] <= qpos[:, None]) & (qpos[:, None] - kpos[None, :] < WINDOW)
        bq, bk, bv = block_grads(q_blk, g_blk, k_span, v_span, visible)
        grad_q = lax.dynamic_update_slice_in_dim(grad_q, bq, q0, 0)
        grad_k = lax.dynamic_update_slice_in_dim(grad_k, lax.dynamic_slice_in_dim(grad_k, q0, span, 0) + bk, q0, 0)
        grad_v = lax.dynamic_update_slice_in_dim(grad_v, lax.dynamic_slice_in_dim(grad_v, q0, span, 0) + bv, q0, 0)
        return grad_q, grad_k, grad_v

    init = (jnp.zeros((SEQ_LEN, HEADS, HEAD_DIM), jnp.bfloat16),
            jnp.zeros((WINDOW + SEQ_LEN, HEADS, HEAD_DIM), jnp.float32),
            jnp.zeros((WINDOW + SEQ_LEN, HEADS, HEAD_DIM), jnp.float32))
    grad_q, grad_k, grad_v = lax.fori_loop(0, SEQ_LEN // QBLOCK, step, init)
    head_k = grad_k[WINDOW:].astype(jnp.bfloat16)
    head_v = grad_v[WINDOW:].astype(jnp.bfloat16)
    out_k = head_k.reshape(SEQ_LEN, KV_HEADS, 2, HEAD_DIM).astype(jnp.float32).sum(axis=2).astype(jnp.bfloat16)
    out_v = head_v.reshape(SEQ_LEN, KV_HEADS, 2, HEAD_DIM).astype(jnp.float32).sum(axis=2).astype(jnp.bfloat16)
    return (grad_q.reshape(SEQ_LEN, HEADS * HEAD_DIM),
            out_k.reshape(SEQ_LEN, KV_HEADS * HEAD_DIM),
            out_v.reshape(SEQ_LEN, KV_HEADS * HEAD_DIM))


def reference(query, key, value, grad_out, tile_start):
    grads_q, grads_k, grads_v = [], [], []
    for seq in range(query.shape[0]):
        one_q, one_k, one_v = one_sequence(query[seq], key[seq], value[seq], grad_out[seq], tile_start[seq])
        grads_q.append(one_q)
        grads_k.append(one_k)
        grads_v.append(one_v)
    return (jnp.stack(grads_q), jnp.stack(grads_k), jnp.stack(grads_v))
```

```python
import math

import jax
import jax.numpy as jnp
from jax import lax
from jax.experimental import pallas as pl
from jax.experimental.pallas import tpu as pltpu
from jax.sharding import PartitionSpec as P

HEADS = 32
KV_HEADS = 16
HEAD_DIM = 128
WINDOW = 1024
TILE = 128
BLOCK = 512
HALF = 256
HEAD_GROUPS = 2

score_scale = 168.0 ** (-0.5)
exp2_scale = score_scale * math.log2(math.e)

VMEM_LIMIT = 48 * 1024 * 1024


def attention_kernel(starts, qg_ref, kv0, kv1, kv2, dq_ref, d0, d1, d2, kt_s, dk_s, dv_s):
    span = [(kv2, 0), (kv2, HALF), (kv1, 0), (kv1, HALF), (kv0, 0), (kv0, HALF)]
    pieces = len(span)
    for n, (ref, lower) in enumerate(span):
        kt_s[n] = ref[0, lower : lower + HALF, :].T
    dk_s[...] = jnp.zeros_like(dk_s)
    dv_s[...] = jnp.zeros_like(dv_s)
    lane = lax.broadcasted_iota(jnp.int32, (1, HALF), 1)
    k_iota = lax.broadcasted_iota(jnp.int32, (HALF, HALF), 0)
    tiles = HALF // TILE
    for j in range(BLOCK // HALF):
        begin = starts[tiles * j]
        first = jnp.full((1, HALF), begin, jnp.int32)
        for t in range(1, tiles):
            first = jnp.where(lane >= t * TILE, starts[tiles * j + t], first)
        q_pos = WINDOW + j * HALF + lane
        count = WINDOW // HALF + 1
        for head in range(2):
            cols = slice(head * HEAD_DIM, (head + 1) * HEAD_DIM)
            rows = slice(j * HALF, (j + 1) * HALF)
            q = qg_ref[0, rows, cols]
            g = qg_ref[1, rows, cols]
            scores = []
            top = None
            for i in range(count):
                ref, lower = span[j + i]
                k = ref[0, lower : lower + HALF, :]
                s = lax.dot_general(
                    k, q, (((1,), (1,)), ((), ())), preferred_element_type=jnp.float32
                )
                k_pos = (j + i) * HALF + k_iota
                visible = k_pos >= first
                if i == 0:
                    visible = visible & (k_pos > q_pos - WINDOW)
                if i == count - 1:
                    visible = visible & (k_pos <= q_pos)
                s = jnp.where(visible, s, -jnp.inf)
                peak = jnp.max(s, axis=0, keepdims=True)
                top = peak if top is None else jnp.maximum(top, peak)
                scores.append(s)
            shift = top * exp2_scale
            weights, grads = [], []
            total, inner = None, None
            for i in range(count):
                ref, lower = span[j + i]
                v = ref[1, lower : lower + HALF, :]
                w = jnp.exp2(scores[i] * exp2_scale - shift)
                dp = lax.dot_general(
                    v, g, (((1,), (1,)), ((), ())), preferred_element_type=jnp.float32
                )
                part = jnp.sum(w, axis=0, keepdims=True)
                mixed = jnp.sum(w * dp, axis=0, keepdims=True)
                total = part if total is None else total + part
                inner = mixed if inner is None else inner + mixed
                weights.append(w)
                grads.append(dp)
            inverse = 1.0 / total
            delta = inner * inverse
            dq_t = None
            for i in range(count):
                at = slice((j + i) * HALF, (j + i + 1) * HALF)
                probs = weights[i] * inverse
                ds = (probs * (grads[i] - delta)).astype(jnp.bfloat16)
                low = probs.astype(jnp.bfloat16)
                dv_s[at, :] += jnp.dot(low, g, preferred_element_type=jnp.float32)
                dk_s[at, :] += jnp.dot(ds, q, preferred_element_type=jnp.float32)
                term = jnp.dot(kt_s[j + i], ds, preferred_element_type=jnp.float32)
                dq_t = term if dq_t is None else dq_t + term
            dq_ref[rows, cols] = (dq_t.T * score_scale).astype(jnp.bfloat16)
    for n, out in enumerate((d2, d1, d0)):
        at = slice(n * BLOCK, (n + 1) * BLOCK)
        out[0] = (dk_s[at, :] * score_scale).astype(jnp.bfloat16)
        out[1] = dv_s[at, :].astype(jnp.bfloat16)


def attention(starts, qg, kv0, kv1, kv2):
    kv_heads = kv0.shape[2] // HEAD_DIM
    both = pl.BlockSpec((2, BLOCK, 2 * HEAD_DIM), lambda h, *_: (0, 0, h))
    wide = pl.BlockSpec((BLOCK, 2 * HEAD_DIM), lambda h, *_: (0, h))
    pair = pl.BlockSpec((2, BLOCK, HEAD_DIM), lambda h, *_: (0, 0, h))
    pair_shape = jax.ShapeDtypeStruct(kv0.shape, jnp.bfloat16)
    keys = WINDOW + BLOCK
    work = kv_heads * 2 * BLOCK * (WINDOW + HALF)
    return pl.pallas_call(
        attention_kernel,
        grid_spec=pltpu.PrefetchScalarGridSpec(
            num_scalar_prefetch=1,
            grid=(kv_heads,),
            in_specs=[both, pair, pair, pair],
            out_specs=[wide, pair, pair, pair],
            scratch_shapes=[
                pltpu.VMEM((keys // HALF, HEAD_DIM, HALF), jnp.bfloat16),
                pltpu.VMEM((keys, HEAD_DIM), jnp.float32),
                pltpu.VMEM((keys, HEAD_DIM), jnp.float32),
            ],
        ),
        out_shape=[jax.ShapeDtypeStruct(qg.shape[1:], jnp.bfloat16)] + [pair_shape] * 3,
        compiler_params=pltpu.CompilerParams(vmem_limit_bytes=VMEM_LIMIT),
        cost_estimate=pl.CostEstimate(
            flops=20 * work * HEAD_DIM, bytes_accessed=8 * qg.size, transcendentals=work
        ),
        name="attention",
    )(starts, qg, kv0, kv1, kv2)


def call_copies(kernel, part, operands, in_specs, out_specs, out_shape, grid=(1,), aliases=None):
    moved = sum(math.prod(shape.shape) for shape in out_shape)
    return pl.pallas_call(
        kernel,
        grid_spec=pltpu.PrefetchScalarGridSpec(
            num_scalar_prefetch=1, grid=grid, in_specs=in_specs, out_specs=out_specs
        ),
        out_shape=out_shape,
        input_output_aliases=aliases or {},
        compiler_params=pltpu.CompilerParams(vmem_limit_bytes=VMEM_LIMIT),
        cost_estimate=pl.CostEstimate(flops=0, bytes_accessed=4 * moved, transcendentals=0),
        name="copies",
    )(part, *operands)


def pack(part, arrays, seq, group):
    rows, width = arrays[0].shape[1], arrays[0].shape[2]
    cols = width // (2 * HEAD_GROUPS)
    count = len(arrays)

    def kernel(_, *refs):
        for n in range(count):
            refs[count][n] = refs[n][0]

    block = pl.BlockSpec((1, rows, cols), lambda _, y: (seq, 0, (1 - y[0]) * HEAD_GROUPS + group))
    shape = (count, rows, cols)
    return call_copies(
        kernel,
        part,
        arrays,
        [block] * count,
        [pl.BlockSpec(shape, lambda *_: (0, 0, 0))],
        [jax.ShapeDtypeStruct(shape, jnp.bfloat16)],
    )[0]


def assemble(part, arrays, came, seq, group):
    rows, width = arrays[0].shape[1], arrays[0].shape[2]
    cols = width // (2 * HEAD_GROUPS)
    count = len(arrays)

    def kernel(part_ref, *refs):
        out = refs[count + 1]
        here = pl.multiple_of(part_ref[0] * rows, rows)
        there = pl.multiple_of((1 - part_ref[0]) * rows, rows)
        for n in range(count):
            out[n, pl.ds(here, rows), :] = refs[n][0]
            out[n, pl.ds(there, rows), :] = refs[count][n]

    block = pl.BlockSpec((1, rows, cols), lambda _, y: (seq, 0, y[0] * HEAD_GROUPS + group))
    shape = (count, 2 * rows, cols)
    return call_copies(
        kernel,
        part,
        list(arrays) + [came],
        [block] * count + [pl.BlockSpec(came.shape, lambda *_: (0, 0, 0))],
        [pl.BlockSpec(shape, lambda *_: (0, 0, 0))],
        [jax.ShapeDtypeStruct(shape, jnp.bfloat16)],
    )[0]


def place(part, kept, came, outs, shape, seq, group):
    count, rows, cols = kept.shape
    old = [] if outs is None else list(outs)

    def kernel(_, kept_ref, came_ref, *refs):
        results = refs[len(old) :]

        @pl.when(pl.program_id(0) == 0)
        def _():
            for n in range(count):
                results[n][0] = kept_ref[n]

        @pl.when(pl.program_id(0) == 1)
        def _():
            for n in range(count):
                results[n][0] = came_ref[n]

    whole = pl.BlockSpec(kept.shape, lambda *_: (0, 0, 0))
    block = pl.BlockSpec(
        (1, rows, cols),
        lambda i, y: (seq, 0, (y[0] + i - 2 * i * y[0]) * HEAD_GROUPS + group),
    )
    return call_copies(
        kernel,
        part,
        [kept, came] + old,
        [whole, whole] + [pl.BlockSpec(memory_space=pl.ANY)] * len(old),
        [block] * count,
        [jax.ShapeDtypeStruct(shape, jnp.bfloat16)] * count,
        grid=(2,),
        aliases={3 + n: n for n in range(len(old))},
    )


def swapped(value):
    pairs = [(i, i ^ 1) for i in range(lax.axis_size("fsdp"))]
    return lax.ppermute(value, "fsdp", pairs)


def shifted(value, by):
    count = lax.axis_size("ctx") * lax.axis_size("fsdp")
    pairs = [(i, i + by) for i in range(count) if 0 <= i + by < count]
    return lax.ppermute(value, ("ctx", "fsdp"), pairs)


def pair_groups(split):
    groups = lax.axis_size("fsdp")
    return [list(range(n, n + split)) for n in range(0, groups, split)]


def to_heads(part, arrays, seq, group, split):
    if split == 2:
        came = swapped(pack(part, arrays, seq, group))
        return assemble(part, arrays, came, seq, group)
    rows, width = arrays[0].shape[1], arrays[0].shape[2]
    cols = width // split // HEAD_GROUPS
    stacked = jnp.stack(
        [a[seq].reshape(rows, split, HEAD_GROUPS, cols)[:, :, group] for a in arrays]
    )
    whole = lax.all_to_all(
        stacked, "fsdp", 2, 1, axis_index_groups=pair_groups(split), tiled=True
    )
    return whole.reshape(len(arrays), split * rows, cols)


def to_tokens(part, block, outs, shape, seq, group, split):
    count, length, cols = block.shape
    rows = length // split
    if split == 2:
        here = part[0]
        send = lax.dynamic_slice_in_dim(block, (1 - here) * rows, rows, 1)
        kept = lax.dynamic_slice_in_dim(block, here * rows, rows, 1)
        return place(part, kept, swapped(send), outs, shape, seq, group)
    if outs is None:
        outs = [jnp.zeros(shape, jnp.bfloat16)] * count
    parts = block.reshape(count, split, rows, cols)
    whole = lax.all_to_all(parts, "fsdp", 1, 1, axis_index_groups=pair_groups(split), tiled=True)
    results = []
    for n in range(count):
        result = outs[n]
        for p in range(split):
            left = (p * HEAD_GROUPS + group) * cols
            result = lax.dynamic_update_slice(result, whole[n, p][None], (seq, 0, left))
        results.append(result)
    return results


def added(one, other):
    return (one.astype(jnp.float32) + other.astype(jnp.float32)).astype(jnp.bfloat16)


def body(query, key, value, grad_out, tile_start):
    seqs, rows, _ = query.shape
    split = BLOCK // rows
    position = lax.axis_index("fsdp")
    part = jnp.full((1,), position % split, jnp.int32)
    blocks = lax.axis_size("fsdp") // split
    block = lax.axis_index("ctx") * blocks + position // split
    per_block = BLOCK // TILE
    tiles = lax.dynamic_slice_in_dim(tile_start, block * per_block, per_block, 1)
    starts = tiles * TILE - (block * BLOCK - WINDOW)
    chunks = [(s, h) for s in range(seqs) for h in range(HEAD_GROUPS)]
    inputs = []
    for seq, group in chunks:
        kv = to_heads(part, (key, value), seq, group, split)
        qg = to_heads(part, (query, grad_out), seq, group, split)
        inputs.append((kv, qg))
    outs_q, outs_kv = None, None
    for (seq, group), (kv0, qg) in zip(chunks, inputs):
        kv1 = shifted(kv0, split)
        kv2 = shifted(kv1, split)
        dq, d0, d1, d2 = attention(starts[seq], qg, kv0, kv1, kv2)
        outs_q = to_tokens(part, dq[None], outs_q, query.shape, seq, group, split)
        back = added(d1, shifted(d2, -split))
        total = added(d0, shifted(back, -split))
        outs_kv = to_tokens(part, total, outs_kv, key.shape, seq, group, split)
    return outs_q[0], outs_kv[0], outs_kv[1]


def solution(mesh):
    tokens = P(None, ("ctx", "fsdp"), None)
    return jax.shard_map(
        body,
        mesh=mesh,
        in_specs=(tokens, tokens, tokens, tokens, P()),
        out_specs=(tokens, tokens, tokens),
        check_vma=False,
    )
```

```python
import functools
import math

import jax
import jax.numpy as jnp
from jax import lax
from jax.experimental import pallas as pl
from jax.experimental.pallas import tpu as pltpu
from jax.sharding import PartitionSpec as P

HEADS = 32
KV_HEADS = 16
HEAD_DIM = 128
WINDOW = 1024
TILE = 128
BLOCK = 512
HALF = 256
HEAD_GROUPS = 2

score_scale = 168.0 ** (-0.5)
exp2_scale = score_scale * math.log2(math.e)

VMEM_LIMIT = 60 * 1024 * 1024
LITTLE = pl.CostEstimate(flops=0, bytes_accessed=1024, transcendentals=0)
ATTENTION = pl.CostEstimate(flops=10000000000, bytes_accessed=1024, transcendentals=0)


def attention_kernel(pieces, starts, part, _, *refs):
    refs = list(refs)

    def take(count):
        taken = refs[:count]
        del refs[:count]
        return taken

    rows = BLOCK // pieces
    q_in = take(2) + take(pieces - 1)
    kv_in = [take(pieces) for _ in range(3)]
    take(1)
    dq_out = take(pieces)
    d_out = take(3)
    q_s, g_s, k_s, v_s, kt_s, dq_s, dk_s, dv_s = refs

    here = part[0]

    def tokens(block, piece):
        place = here if piece == 0 else 1 - here
        return pl.ds(pl.multiple_of(block * BLOCK + place * rows, rows), rows)

    q_s[tokens(0, 0), :] = q_in[0][0]
    g_s[tokens(0, 0), :] = q_in[1][0]
    for i in range(1, pieces):
        q_s[tokens(0, i), :] = q_in[1 + i][0]
        g_s[tokens(0, i), :] = q_in[1 + i][1]
    for block, given in zip((2, 1, 0), kv_in):
        for i in range(pieces):
            k_s[tokens(block, i), :] = given[i][0, 0]
            v_s[tokens(block, i), :] = given[i][0, 1]
    for n in range((WINDOW + BLOCK) // HALF):
        kt_s[n] = k_s[n * HALF : (n + 1) * HALF, :].T
    dk_s[...] = jnp.zeros_like(dk_s)
    dv_s[...] = jnp.zeros_like(dv_s)
    lane = lax.broadcasted_iota(jnp.int32, (1, HALF), 1)
    k_iota = lax.broadcasted_iota(jnp.int32, (HALF, HALF), 0)
    tiles = HALF // TILE
    for j in range(BLOCK // HALF):
        first = jnp.full((1, HALF), starts[tiles * j], jnp.int32)
        for t in range(1, tiles):
            first = jnp.where(lane >= t * TILE, starts[tiles * j + t], first)
        q_pos = WINDOW + j * HALF + lane
        count = WINDOW // HALF + 1
        for head in range(2):
            cols = slice(head * HEAD_DIM, (head + 1) * HEAD_DIM)
            at_q = slice(j * HALF, (j + 1) * HALF)
            q = q_s[at_q, cols]
            g = g_s[at_q, cols]
            scores = []
            top = None
            for i in range(count):
                at = slice((j + i) * HALF, (j + i + 1) * HALF)
                s = lax.dot_general(
                    k_s[at, :], q, (((1,), (1,)), ((), ())), preferred_element_type=jnp.float32
                )
                k_pos = (j + i) * HALF + k_iota
                visible = k_pos >= first
                if i == 0:
                    visible = visible & (k_pos > q_pos - WINDOW)
                if i == count - 1:
                    visible = visible & (k_pos <= q_pos)
                s = jnp.where(visible, s, -jnp.inf)
                peak = jnp.max(s, axis=0, keepdims=True)
                top = peak if top is None else jnp.maximum(top, peak)
                scores.append(s)
            shift = top * exp2_scale
            weights, grads = [], []
            total, inner = None, None
            for i in range(count):
                at = slice((j + i) * HALF, (j + i + 1) * HALF)
                w = jnp.exp2(scores[i] * exp2_scale - shift)
                dp = lax.dot_general(
                    v_s[at, :], g, (((1,), (1,)), ((), ())), preferred_element_type=jnp.float32
                )
                part_sum = jnp.sum(w, axis=0, keepdims=True)
                mixed = jnp.sum(w * dp, axis=0, keepdims=True)
                total = part_sum if total is None else total + part_sum
                inner = mixed if inner is None else inner + mixed
                weights.append(w)
                grads.append(dp)
            inverse = 1.0 / total
            delta = inner * inverse
            dq_t = None
            for i in range(count):
                at = slice((j + i) * HALF, (j + i + 1) * HALF)
                probs = weights[i] * inverse
                ds = (probs * (grads[i] - delta)).astype(jnp.bfloat16)
                low = probs.astype(jnp.bfloat16)
                dv_s[at, :] += jnp.dot(low, g, preferred_element_type=jnp.float32)
                dk_s[at, :] += jnp.dot(ds, q, preferred_element_type=jnp.float32)
                term = jnp.dot(kt_s[j + i], ds, preferred_element_type=jnp.float32)
                dq_t = term if dq_t is None else dq_t + term
            dq_s[at_q, cols] = (dq_t.T * score_scale).astype(jnp.bfloat16)
    for i in range(pieces):
        dq_out[i][0] = dq_s[tokens(0, i), :]
        for block, out in zip((2, 1, 0), d_out):
            out[i, 0] = (dk_s[tokens(block, i), :] * score_scale).astype(jnp.bfloat16)
            out[i, 1] = dv_s[tokens(block, i), :].astype(jnp.bfloat16)


def attention(token, starts, part, q_own, q_came, blocks, cols):
    pieces = len(blocks[0])
    rows = BLOCK // pieces
    heads = cols // HEAD_DIM
    wide = 2 * HEAD_DIM
    keys = WINDOW + BLOCK
    bf16 = jnp.bfloat16

    def piece(lead, width):
        return pl.BlockSpec((*lead, rows, width), lambda h, *_: (0,) * (len(lead) + 1) + (h,))

    moved = piece((pieces, 2), HEAD_DIM)
    flat = [given for block in blocks for given in block]
    operands = [a for a, _ in q_own] + q_came + [a for a, _ in flat]
    in_specs = [pl.BlockSpec((1, rows, wide), index) for _, index in q_own]
    in_specs += [piece((2,), wide)] * len(q_came)
    in_specs += [
        pl.BlockSpec((1, 2, rows, HEAD_DIM), lambda h, *_, at=at: (at, 0, 0, h)) for _, at in flat
    ]
    anywhere = pl.BlockSpec(memory_space=pl.ANY)
    return pl.pallas_call(
        functools.partial(attention_kernel, pieces),
        grid_spec=pltpu.PrefetchScalarGridSpec(
            num_scalar_prefetch=2,
            grid=(heads,),
            in_specs=[anywhere] + in_specs,
            out_specs=[anywhere] + [piece((1,), wide)] * pieces + [moved] * 3,
            scratch_shapes=[
                pltpu.VMEM((BLOCK, wide), bf16),
                pltpu.VMEM((BLOCK, wide), bf16),
                pltpu.VMEM((keys, HEAD_DIM), bf16),
                pltpu.VMEM((keys, HEAD_DIM), bf16),
                pltpu.VMEM((keys // HALF, HEAD_DIM, HALF), bf16),
                pltpu.VMEM((BLOCK, wide), bf16),
                pltpu.VMEM((keys, HEAD_DIM), jnp.float32),
                pltpu.VMEM((keys, HEAD_DIM), jnp.float32),
            ],
        ),
        out_shape=[jax.ShapeDtypeStruct(token.shape, token.dtype)]
        + [jax.ShapeDtypeStruct((1, rows, 2 * cols), bf16)] * pieces
        + [jax.ShapeDtypeStruct((pieces, 2, rows, cols), bf16)] * 3,
        input_output_aliases={2: 0},
        compiler_params=pltpu.CompilerParams(vmem_limit_bytes=VMEM_LIMIT),
        cost_estimate=ATTENTION,
        name="attention",
    )(starts, part, token, *operands)


def call_copies(kernel, token, part, operands, in_specs, out_specs, out_shape, grid=(1,), aliases=None):
    ins, outs = len(operands), len(out_shape)

    def body(part_ref, _, *refs):
        kernel(part_ref, *refs[:ins], *refs[ins + 1 :])

    anywhere = pl.BlockSpec(memory_space=pl.ANY)
    results = pl.pallas_call(
        body,
        grid_spec=pltpu.PrefetchScalarGridSpec(
            num_scalar_prefetch=1,
            grid=grid,
            in_specs=[anywhere] + in_specs,
            out_specs=[anywhere] + out_specs,
        ),
        out_shape=[jax.ShapeDtypeStruct(token.shape, token.dtype)] + out_shape,
        input_output_aliases={1: 0, **{i + 1: o + 1 for i, o in (aliases or {}).items()}},
        compiler_params=pltpu.CompilerParams(vmem_limit_bytes=VMEM_LIMIT),
        cost_estimate=LITTLE,
        name="copies",
    )(part, token, *operands)
    return results[0], results[1:]


def pack(token, part, arrays, seq, group, groups, both):
    rows, width = arrays[0].shape[1], arrays[0].shape[2]
    cols = width // (2 * groups)
    count = len(arrays)
    results = 2 if both else 1

    def kernel(_, *refs):
        for n in range(count * results):
            refs[count * results + n // count][n % count] = refs[n][0]

    theirs = pl.BlockSpec((1, rows, cols), lambda _, y: (seq, 0, (1 - y[0]) * groups + group))
    ours = pl.BlockSpec((1, rows, cols), lambda _, y: (seq, 0, y[0] * groups + group))
    shape = (count, rows, cols)
    return call_copies(
        kernel,
        token,
        part,
        list(arrays) * results,
        [theirs] * count + [ours] * (count * (results - 1)),
        [pl.BlockSpec(shape, lambda *_: (0, 0, 0))] * results,
        [jax.ShapeDtypeStruct(shape, jnp.bfloat16)] * results,
    )


def assemble(token, part, arrays, came, seq, group, groups):
    rows, width = arrays[0].shape[1], arrays[0].shape[2]
    cols = width // (2 * groups)
    count = len(arrays)

    def kernel(_, *refs):
        out = refs[count + 1]
        for n in range(count):
            out[0, n] = refs[n][0]
            out[1, n] = refs[count][n]

    ours = pl.BlockSpec((1, rows, cols), lambda _, y: (seq, 0, y[0] * groups + group))
    shape = (2, count, rows, cols)
    token, results = call_copies(
        kernel,
        token,
        part,
        list(arrays) + [came],
        [ours] * count + [pl.BlockSpec(came.shape, lambda *_: (0, 0, 0))],
        [pl.BlockSpec(shape, lambda *_: (0, 0, 0, 0))],
        [jax.ShapeDtypeStruct(shape, jnp.bfloat16)],
    )
    return token, results[0]


def sums(token, part, one, other, apart):
    pieces, count, rows, cols = one.shape

    def kernel(_, one_ref, other_ref, *outs):
        for i in range(pieces):
            value = added(one_ref[i], other_ref[i])
            if apart:
                outs[i][...] = value
            else:
                outs[0][i] = value

    block = pl.BlockSpec((pieces, 1, rows, cols), lambda n, _: (0, n, 0, 0))
    shapes = [one.shape]
    out_specs = [block]
    if apart:
        shapes = [one.shape[1:]] * pieces
        out_specs = [pl.BlockSpec((1, rows, cols), lambda n, _: (n, 0, 0))] * pieces
    token, results = call_copies(
        kernel,
        token,
        part,
        [one, other],
        [block, block],
        out_specs,
        [jax.ShapeDtypeStruct(shape, jnp.bfloat16) for shape in shapes],
        grid=(count,),
    )
    return token, results if apart else results[0]


def joined(token, part, arrays):
    count, rows, cols = arrays[0].shape
    pieces = len(arrays)

    def kernel(_, *refs):
        for i in range(pieces):
            refs[pieces][i] = refs[i][...]

    token, results = call_copies(
        kernel,
        token,
        part,
        arrays,
        [pl.BlockSpec((1, rows, cols), lambda n, _: (n, 0, 0))] * pieces,
        [pl.BlockSpec((pieces, 1, rows, cols), lambda n, _: (0, n, 0, 0))],
        [jax.ShapeDtypeStruct((pieces, count, rows, cols), jnp.bfloat16)],
        grid=(count,),
    )
    return token, results[0]


def place(token, part, ours, theirs, outs, shape, seq, group, groups):
    count, rows, cols = ours[0].shape
    terms = len(ours)
    old = [] if outs is None else list(outs)

    def kernel(_, *refs):
        results = refs[2 * terms + len(old) :]
        for step in range(2):

            @pl.when(pl.program_id(0) == step)
            def _():
                given = refs[step * terms : (step + 1) * terms]
                for n in range(count):
                    value = given[0][n]
                    if terms == 2:
                        value = added(value, given[1][n])
                    results[n][0] = value

    whole = pl.BlockSpec((count, rows, cols), lambda *_: (0, 0, 0))
    block = pl.BlockSpec(
        (1, rows, cols), lambda i, y: (seq, 0, (y[0] + i - 2 * i * y[0]) * groups + group)
    )
    return call_copies(
        kernel,
        token,
        part,
        list(ours) + list(theirs) + old,
        [whole] * (2 * terms) + [pl.BlockSpec(memory_space=pl.ANY)] * len(old),
        [block] * count,
        [jax.ShapeDtypeStruct(shape, jnp.bfloat16)] * count,
        grid=(2,),
        aliases={2 * terms + 1 + n: n for n in range(len(old))},
    )


def swapped(value):
    pairs = [(i, i ^ 1) for i in range(lax.axis_size("fsdp"))]
    return lax.ppermute(value, "fsdp", pairs)


def shifted(value, by, across=0):
    count = lax.axis_size("ctx") * lax.axis_size("fsdp")
    pairs = [(i, (i + by) ^ across) for i in range(count) if 0 <= i + by < count]
    return lax.ppermute(value, ("ctx", "fsdp"), pairs)


def regrouped(value, split_axis, concat_axis, split):
    groups = lax.axis_size("fsdp")
    members = [list(range(n, n + split)) for n in range(0, groups, split)]
    return lax.all_to_all(
        value, "fsdp", split_axis, concat_axis, axis_index_groups=members, tiled=True
    )


def to_heads(arrays, seq, group, groups, split):
    rows, width = arrays[0].shape[1], arrays[0].shape[2]
    cols = width // split // groups
    send = jnp.stack([a[seq].reshape(rows, split, groups, cols)[:, :, group] for a in arrays])
    return regrouped(send, 2, 1, split).reshape(len(arrays), split * rows, cols)


def to_tokens(value, outs, shape, seq, group, groups, split):
    count, length, cols = value.shape
    rows = length // split
    whole = regrouped(value.reshape(count, split, rows, cols), 1, 1, split)
    results = []
    for n in range(count):
        result = jnp.zeros(shape, jnp.bfloat16) if outs is None else outs[n]
        for p in range(split):
            left = (p * groups + group) * cols
            result = lax.dynamic_update_slice(result, whole[n, p][None], (seq, 0, left))
        results.append(result)
    return results


def tie(one, other):
    return lax.optimization_barrier((one, other))


def added(one, other):
    return (one.astype(jnp.float32) + other.astype(jnp.float32)).astype(jnp.bfloat16)


def body(query, key, value, grad_out, tile_start):
    seqs, rows, _ = query.shape
    split = BLOCK // rows
    position = lax.axis_index("fsdp")
    blocks = lax.axis_size("fsdp") // split
    block = lax.axis_index("ctx") * blocks + position // split
    per_block = BLOCK // TILE
    tiles = lax.dynamic_slice_in_dim(tile_start, block * per_block, per_block, 1)
    starts = tiles * TILE - (block * BLOCK - WINDOW)
    paired = split == 2
    part = jnp.full((1,), position % 2 if paired else 0, jnp.int32)
    groups = min(HEAD_GROUPS, KV_HEADS // split)
    cols = KV_HEADS * HEAD_DIM // split // groups
    heads = cols // HEAD_DIM
    pieces = 2 if paired else 1
    chunks = [(s, h, groups) for s in range(seqs) for h in range(groups)]
    count = len(chunks)
    kv_arrays, qg_arrays = (key, value), (query, grad_out)
    straight = [paired and c == count - 1 for c in range(count)]
    kv_send, kv_came, qg_came, q_own, kv0, kv1, kv2 = ([None] * count for _ in range(7))
    dq, dq_came, d0, d1, d2, d0_came = ([None] * count for _ in range(6))
    d1_came, back, d0_more, total, total_came = ([None] * count for _ in range(5))
    outs_q, outs_kv = None, None
    token = jnp.zeros((8, 128), jnp.float32)

    def pack_kv(c):
        nonlocal token
        if not paired:
            kv0[c] = to_heads(kv_arrays, *chunks[c], split)[None]
            return
        token, results = pack(token, part, kv_arrays, *chunks[c], c == 0)
        kv_send[c] = results[0]
        if c == 0:
            kv0[c] = (results[1], results[0])

    def swap_kv(c):
        nonlocal token
        if paired:
            kv_send[c], token = tie(kv_send[c], token)
            with jax.named_scope(f"kv_swap_{c}"):
                kv_came[c] = swapped(kv_send[c])

    def wait_kv(c):
        nonlocal token
        if paired:
            kv_came[c], token = tie(kv_came[c], token)

    def swap_qg(c):
        nonlocal token
        if not paired:
            qg = to_heads(qg_arrays, *chunks[c], split)
            q_own[c] = [(qg, lambda h, *_, n=n: (n, 0, h)) for n in range(2)]
            return
        seq, group, _ = chunks[c]

        def own(h, _, y):
            return (seq, 0, (y[0] * groups + group) * heads + h)

        q_own[c] = [(a, own) for a in qg_arrays]
        token, results = pack(token, part, qg_arrays, *chunks[c], False)
        with jax.named_scope(f"qg_swap_{c}"):
            qg_came[c] = swapped(results[0])

    def wait_qg(c):
        nonlocal token
        if paired:
            qg_came[c], token = tie(qg_came[c], token)

    def hop_1(c):
        nonlocal token
        if paired and c > 0:
            token, kv0[c] = assemble(token, part, kv_arrays, kv_came[c], *chunks[c])
        with jax.named_scope(f"kv_hop_1_{c}"):
            if paired and c == 0:
                kv1[c] = [shifted(a, split, across) for across, a in enumerate(kv0[c])]
            else:
                kv1[c] = shifted(kv0[c], split)

    def hop_2(c):
        nonlocal token
        if paired and c == 0:
            token, kv1[c] = joined(token, part, kv1[c])
        else:
            kv1[c], token = tie(kv1[c], token)
        with jax.named_scope(f"kv_hop_2_{c}"):
            kv2[c] = shifted(kv1[c], split)

    def attend(c):
        nonlocal token
        if paired and c == 0:
            blocks = [[(kv0[c][0][None], 0), (kv_came[c][None], 0)]]
        else:
            blocks = [[(kv0[c], i) for i in range(pieces)]]
        blocks += [[(a, i) for i in range(pieces)] for a in (kv1[c], kv2[c])]
        came = [qg_came[c]] if paired else []
        token, *results = attention(
            token, starts[chunks[c][0]], part, q_own[c], came, blocks, cols
        )
        dq[c] = results[:-3]
        d0[c], d1[c], d2[c] = results[-3:]

    def wait_hop(c):
        nonlocal token
        kv2[c], token = tie(kv2[c], token)

    def return_1(c):
        nonlocal token
        d2[c], token = tie(d2[c], token)
        with jax.named_scope(f"back_1_{c}"):
            d1_came[c] = shifted(d2[c], -split)

    def return_2(c):
        nonlocal token
        apart = straight[c]
        token, back[c] = sums(token, part, d1[c], d1_came[c], apart)
        with jax.named_scope(f"back_2_{c}"):
            if apart:
                d0_more[c] = [shifted(a, -split, across) for across, a in enumerate(back[c])]
            else:
                d0_more[c] = shifted(back[c], -split)

    def swap_grad_kv(c):
        nonlocal token
        if straight[c]:
            send, token = tie(d0[c][1], token)
            with jax.named_scope(f"grad_kv_swap_{c}"):
                d0_came[c] = swapped(send)
        elif paired:
            token, total[c] = sums(token, part, d0[c], d0_more[c], True)
            with jax.named_scope(f"grad_kv_swap_{c}"):
                total_came[c] = swapped(total[c][1])

    def wait_grad_kv(c):
        nonlocal token
        if straight[c]:
            d0_came[c], token = tie(d0_came[c], token)

    def swap_grad_q(c):
        nonlocal token
        if paired:
            dq[c][1], token = tie(dq[c][1], token)
            with jax.named_scope(f"grad_q_swap_{c}"):
                dq_came[c] = swapped(dq[c][1])

    def put_q(c):
        nonlocal token, outs_q
        if paired:
            token, outs_q = place(
                token, part, dq[c][:1], [dq_came[c]], outs_q, query.shape, *chunks[c]
            )
        else:
            outs_q = to_tokens(dq[c][0], outs_q, query.shape, *chunks[c], split)

    def put_kv(c):
        nonlocal token, outs_kv
        if not paired:
            token, total[c] = sums(token, part, d0[c], d0_more[c], True)
            outs_kv = to_tokens(total[c][0], outs_kv, key.shape, *chunks[c], split)
            return
        if straight[c]:
            ours, theirs = [d0[c][0], d0_more[c][0]], [d0_came[c], d0_more[c][1]]
        else:
            ours, theirs = total[c][:1], [total_came[c]]
        token, outs_kv = place(token, part, ours, theirs, outs_kv, key.shape, *chunks[c])

    stages = [pack_kv, swap_kv, swap_qg, hop_1, hop_2, attend, return_1, return_2]
    stages += [swap_grad_kv, swap_grad_q, put_q, put_kv]
    plan = [(stage, c) for c in range(count) for stage in stages]
    if count == 4:
        plan = [
            (pack_kv, 0), (hop_1, 0), (pack_kv, 1), (swap_kv, 1), (pack_kv, 2), (pack_kv, 3),
            (hop_1, 1), (swap_kv, 2), (swap_kv, 0), (hop_2, 0), (hop_1, 2), (swap_qg, 0),
            (wait_kv, 0), (swap_kv, 3), (hop_2, 1), (hop_1, 3), (wait_qg, 0), (swap_qg, 1),
            (hop_2, 2), (attend, 0), (hop_2, 3), (wait_qg, 1), (swap_qg, 2), (attend, 1),
            (return_1, 0), (wait_qg, 2), (swap_qg, 3), (attend, 2), (wait_hop, 3), (return_1, 1),
            (wait_qg, 3), (return_2, 0), (swap_grad_q, 0), (attend, 3), (return_1, 2), (put_q, 0),
            (swap_grad_q, 1), (return_2, 1), (return_1, 3), (swap_grad_kv, 0), (put_q, 1),
            (swap_grad_q, 2), (return_2, 2), (put_kv, 0), (put_q, 2), (swap_grad_kv, 3),
            (swap_grad_q, 3), (swap_grad_kv, 1), (put_q, 3), (wait_grad_kv, 3), (return_2, 3),
            (put_kv, 1), (swap_grad_kv, 2), (put_kv, 3), (put_kv, 2),
        ]
    for stage, c in plan:
        stage(c)
    return outs_q[0], outs_kv[0], outs_kv[1]


def solution(mesh):
    tokens = P(None, ("ctx", "fsdp"), None)
    return jax.shard_map(
        body,
        mesh=mesh,
        in_specs=(tokens, tokens, tokens, tokens, P()),
        out_specs=(tokens, tokens, tokens),
        check_vma=False,
    )
```

```python
import functools
import math

import jax
import jax.numpy as jnp
from jax import lax
from jax.experimental import pallas as pl
from jax.experimental.pallas import tpu as pltpu
from jax.sharding import PartitionSpec as P

HEADS = 32
KV_HEADS = 16
HEAD_DIM = 128
WINDOW = 1024
TILE = 128
BLOCK = 512
HALF = 256
HEAD_GROUPS = 2

score_scale = 168.0 ** (-0.5)
exp2_scale = score_scale * math.log2(math.e)

VMEM_LIMIT = 60 * 1024 * 1024
LAST_GRANT = 63 * 1024 * 1024 + 512 * 1024
LITTLE = pl.CostEstimate(flops=0, bytes_accessed=1024, transcendentals=0)
ATTENTION = pl.CostEstimate(flops=10000000000, bytes_accessed=1024, transcendentals=0)


def attention_kernel(pieces, starts, part, _, *refs):
    refs = list(refs)

    def take(count):
        taken = refs[:count]
        del refs[:count]
        return taken

    rows = BLOCK // pieces
    q_in = take(2) + take(pieces - 1)
    kv_in = [take(pieces) for _ in range(3)]
    take(1)
    dq_out = take(pieces)
    d_out = take(3)
    q_s, g_s, k_s, v_s, kt_s, dq_s, dk_s, dv_s = refs

    here = part[0]

    def tokens(block, piece):
        place = here if piece == 0 else 1 - here
        return pl.ds(pl.multiple_of(block * BLOCK + place * rows, rows), rows)

    q_s[tokens(0, 0), :] = q_in[0][0]
    g_s[tokens(0, 0), :] = q_in[1][0]
    for i in range(1, pieces):
        q_s[tokens(0, i), :] = q_in[1 + i][0]
        g_s[tokens(0, i), :] = q_in[1 + i][1]
    for block, given in zip((2, 1, 0), kv_in):
        for i in range(pieces):
            k_s[tokens(block, i), :] = given[i][0, 0]
            v_s[tokens(block, i), :] = given[i][0, 1]
    for n in range((WINDOW + BLOCK) // HALF):
        kt_s[n] = k_s[n * HALF : (n + 1) * HALF, :].T
    dk_s[...] = jnp.zeros_like(dk_s)
    dv_s[...] = jnp.zeros_like(dv_s)
    lane = lax.broadcasted_iota(jnp.int32, (1, HALF), 1)
    k_iota = lax.broadcasted_iota(jnp.int32, (HALF, HALF), 0)
    tiles = HALF // TILE
    for j in range(BLOCK // HALF):
        first = jnp.full((1, HALF), starts[tiles * j], jnp.int32)
        for t in range(1, tiles):
            first = jnp.where(lane >= t * TILE, starts[tiles * j + t], first)
        q_pos = WINDOW + j * HALF + lane
        count = WINDOW // HALF + 1
        for head in range(2):
            cols = slice(head * HEAD_DIM, (head + 1) * HEAD_DIM)
            at_q = slice(j * HALF, (j + 1) * HALF)
            q = q_s[at_q, cols]
            g = g_s[at_q, cols]
            scores = []
            top = None
            for i in range(count):
                at = slice((j + i) * HALF, (j + i + 1) * HALF)
                s = lax.dot_general(
                    k_s[at, :], q, (((1,), (1,)), ((), ())), preferred_element_type=jnp.float32
                )
                k_pos = (j + i) * HALF + k_iota
                visible = k_pos >= first
                if i == 0:
                    visible = visible & (k_pos > q_pos - WINDOW)
                if i == count - 1:
                    visible = visible & (k_pos <= q_pos)
                s = jnp.where(visible, s, -jnp.inf)
                peak = jnp.max(s, axis=0, keepdims=True)
                top = peak if top is None else jnp.maximum(top, peak)
                scores.append(s)
            shift = top * exp2_scale
            weights, grads = [], []
            total, inner = None, None
            for i in range(count):
                at = slice((j + i) * HALF, (j + i + 1) * HALF)
                w = jnp.exp2(scores[i] * exp2_scale - shift)
                dp = lax.dot_general(
                    v_s[at, :], g, (((1,), (1,)), ((), ())), preferred_element_type=jnp.float32
                )
                part_sum = jnp.sum(w, axis=0, keepdims=True)
                mixed = jnp.sum(w * dp, axis=0, keepdims=True)
                total = part_sum if total is None else total + part_sum
                inner = mixed if inner is None else inner + mixed
                weights.append(w)
                grads.append(dp)
            inverse = 1.0 / total
            delta = inner * inverse
            dq_t = None
            for i in range(count):
                at = slice((j + i) * HALF, (j + i + 1) * HALF)
                probs = weights[i] * inverse
                ds = (probs * (grads[i] - delta)).astype(jnp.bfloat16)
                low = probs.astype(jnp.bfloat16)
                dv_s[at, :] += jnp.dot(low, g, preferred_element_type=jnp.float32)
                dk_s[at, :] += jnp.dot(ds, q, preferred_element_type=jnp.float32)
                term = jnp.dot(kt_s[j + i], ds, preferred_element_type=jnp.float32)
                dq_t = term if dq_t is None else dq_t + term
            dq_s[at_q, cols] = (dq_t.T * score_scale).astype(jnp.bfloat16)
    for i in range(pieces):
        dq_out[i][0] = dq_s[tokens(0, i), :]
        for block, out in zip((2, 1, 0), d_out):
            out[i, 0] = (dk_s[tokens(block, i), :] * score_scale).astype(jnp.bfloat16)
            out[i, 1] = dv_s[tokens(block, i), :].astype(jnp.bfloat16)


def attention(token, starts, part, q_own, q_came, blocks, cols):
    pieces = len(blocks[0])
    rows = BLOCK // pieces
    heads = cols // HEAD_DIM
    wide = 2 * HEAD_DIM
    keys = WINDOW + BLOCK
    bf16 = jnp.bfloat16

    def piece(lead, width):
        return pl.BlockSpec((*lead, rows, width), lambda h, *_: (0,) * (len(lead) + 1) + (h,))

    moved = piece((pieces, 2), HEAD_DIM)
    flat = [given for block in blocks for given in block]
    operands = [a for a, _ in q_own] + q_came + [a for a, _ in flat]
    in_specs = [pl.BlockSpec((1, rows, wide), index) for _, index in q_own]
    in_specs += [piece((2,), wide)] * len(q_came)
    in_specs += [
        pl.BlockSpec((1, 2, rows, HEAD_DIM), lambda h, *_, at=at: (at, 0, 0, h)) for _, at in flat
    ]
    anywhere = pl.BlockSpec(memory_space=pl.ANY)
    return pl.pallas_call(
        functools.partial(attention_kernel, pieces),
        grid_spec=pltpu.PrefetchScalarGridSpec(
            num_scalar_prefetch=2,
            grid=(heads,),
            in_specs=[anywhere] + in_specs,
            out_specs=[anywhere] + [piece((1,), wide)] * pieces + [moved] * 3,
            scratch_shapes=[
                pltpu.VMEM((BLOCK, wide), bf16),
                pltpu.VMEM((BLOCK, wide), bf16),
                pltpu.VMEM((keys, HEAD_DIM), bf16),
                pltpu.VMEM((keys, HEAD_DIM), bf16),
                pltpu.VMEM((keys // HALF, HEAD_DIM, HALF), bf16),
                pltpu.VMEM((BLOCK, wide), bf16),
                pltpu.VMEM((keys, HEAD_DIM), jnp.float32),
                pltpu.VMEM((keys, HEAD_DIM), jnp.float32),
            ],
        ),
        out_shape=[jax.ShapeDtypeStruct(token.shape, token.dtype)]
        + [jax.ShapeDtypeStruct((1, rows, 2 * cols), bf16)] * pieces
        + [jax.ShapeDtypeStruct((pieces, 2, rows, cols), bf16)] * 3,
        input_output_aliases={2: 0},
        compiler_params=pltpu.CompilerParams(vmem_limit_bytes=VMEM_LIMIT),
        cost_estimate=ATTENTION,
        name="attention",
    )(starts, part, token, *operands)


def call_copies(
    kernel, token, part, operands, in_specs, out_specs, out_shape, grid=(1,), aliases=None, grant=None
):
    ins, outs = len(operands), len(out_shape)

    def body(part_ref, _, *refs):
        kernel(part_ref, *refs[:ins], *refs[ins + 1 :])

    anywhere = pl.BlockSpec(memory_space=pl.ANY)
    results = pl.pallas_call(
        body,
        grid_spec=pltpu.PrefetchScalarGridSpec(
            num_scalar_prefetch=1,
            grid=grid,
            in_specs=[anywhere] + in_specs,
            out_specs=[anywhere] + out_specs,
        ),
        out_shape=[jax.ShapeDtypeStruct(token.shape, token.dtype)] + out_shape,
        input_output_aliases={1: 0, **{i + 1: o + 1 for i, o in (aliases or {}).items()}},
        compiler_params=pltpu.CompilerParams(vmem_limit_bytes=grant or VMEM_LIMIT),
        cost_estimate=LITTLE,
        name="copies",
    )(part, token, *operands)
    return results[0], results[1:]


def pack(token, part, arrays, seq, group, groups, both):
    rows, width = arrays[0].shape[1], arrays[0].shape[2]
    cols = width // (2 * groups)
    count = len(arrays)
    results = 2 if both else 1

    def kernel(_, *refs):
        for n in range(count * results):
            refs[count * results + n // count][n % count] = refs[n][0]

    theirs = pl.BlockSpec((1, rows, cols), lambda _, y: (seq, 0, (1 - y[0]) * groups + group))
    ours = pl.BlockSpec((1, rows, cols), lambda _, y: (seq, 0, y[0] * groups + group))
    shape = (count, rows, cols)
    return call_copies(
        kernel,
        token,
        part,
        list(arrays) * results,
        [theirs] * count + [ours] * (count * (results - 1)),
        [pl.BlockSpec(shape, lambda *_: (0, 0, 0))] * results,
        [jax.ShapeDtypeStruct(shape, jnp.bfloat16)] * results,
    )


def assemble(token, part, arrays, came, seq, group, groups):
    rows, width = arrays[0].shape[1], arrays[0].shape[2]
    cols = width // (2 * groups)
    count = len(arrays)

    def kernel(_, *refs):
        out = refs[count + 1]
        for n in range(count):
            out[0, n] = refs[n][0]
            out[1, n] = refs[count][n]

    ours = pl.BlockSpec((1, rows, cols), lambda _, y: (seq, 0, y[0] * groups + group))
    shape = (2, count, rows, cols)
    token, results = call_copies(
        kernel,
        token,
        part,
        list(arrays) + [came],
        [ours] * count + [pl.BlockSpec(came.shape, lambda *_: (0, 0, 0))],
        [pl.BlockSpec(shape, lambda *_: (0, 0, 0, 0))],
        [jax.ShapeDtypeStruct(shape, jnp.bfloat16)],
    )
    return token, results[0]


def sums(token, part, one, other, apart):
    pieces, count, rows, cols = one.shape

    def kernel(_, one_ref, other_ref, *outs):
        for i in range(pieces):
            value = added(one_ref[i], other_ref[i])
            if apart:
                outs[i][...] = value
            else:
                outs[0][i] = value

    block = pl.BlockSpec((pieces, 1, rows, cols), lambda n, _: (0, n, 0, 0))
    shapes = [one.shape]
    out_specs = [block]
    if apart:
        shapes = [one.shape[1:]] * pieces
        out_specs = [pl.BlockSpec((1, rows, cols), lambda n, _: (n, 0, 0))] * pieces
    token, results = call_copies(
        kernel,
        token,
        part,
        [one, other],
        [block, block],
        out_specs,
        [jax.ShapeDtypeStruct(shape, jnp.bfloat16) for shape in shapes],
        grid=(count,),
    )
    return token, results if apart else results[0]


def joined(token, part, arrays):
    count, rows, cols = arrays[0].shape
    pieces = len(arrays)

    def kernel(_, *refs):
        for i in range(pieces):
            refs[pieces][i] = refs[i][...]

    token, results = call_copies(
        kernel,
        token,
        part,
        arrays,
        [pl.BlockSpec((1, rows, cols), lambda n, _: (n, 0, 0))] * pieces,
        [pl.BlockSpec((pieces, 1, rows, cols), lambda n, _: (0, n, 0, 0))],
        [jax.ShapeDtypeStruct((pieces, count, rows, cols), jnp.bfloat16)],
        grid=(count,),
    )
    return token, results[0]


def place(token, part, ours, theirs, outs, shape, seq, group, groups, grant=None):
    count, rows, cols = ours[0].shape
    terms = len(ours)
    old = [] if outs is None else list(outs)

    def kernel(_, *refs):
        results = refs[2 * terms + len(old) :]
        for step in range(2):

            @pl.when(pl.program_id(0) == step)
            def _():
                given = refs[step * terms : (step + 1) * terms]
                for n in range(count):
                    value = given[0][n]
                    if terms == 2:
                        value = added(value, given[1][n])
                    results[n][0] = value

    whole = pl.BlockSpec((count, rows, cols), lambda *_: (0, 0, 0))
    block = pl.BlockSpec(
        (1, rows, cols), lambda i, y: (seq, 0, (y[0] + i - 2 * i * y[0]) * groups + group)
    )
    return call_copies(
        kernel,
        token,
        part,
        list(ours) + list(theirs) + old,
        [whole] * (2 * terms) + [pl.BlockSpec(memory_space=pl.ANY)] * len(old),
        [block] * count,
        [jax.ShapeDtypeStruct(shape, jnp.bfloat16)] * count,
        grid=(2,),
        aliases={2 * terms + 1 + n: n for n in range(len(old))},
        grant=grant,
    )


def swapped(value):
    pairs = [(i, i ^ 1) for i in range(lax.axis_size("fsdp"))]
    return lax.ppermute(value, "fsdp", pairs)


def shifted(value, by, across=0):
    count = lax.axis_size("ctx") * lax.axis_size("fsdp")
    pairs = [(i, (i + by) ^ across) for i in range(count) if 0 <= i + by < count]
    return lax.ppermute(value, ("ctx", "fsdp"), pairs)


def regrouped(value, split_axis, concat_axis, split):
    groups = lax.axis_size("fsdp")
    members = [list(range(n, n + split)) for n in range(0, groups, split)]
    return lax.all_to_all(
        value, "fsdp", split_axis, concat_axis, axis_index_groups=members, tiled=True
    )


def to_heads(arrays, seq, group, groups, split):
    rows, width = arrays[0].shape[1], arrays[0].shape[2]
    cols = width // split // groups
    send = jnp.stack([a[seq].reshape(rows, split, groups, cols)[:, :, group] for a in arrays])
    return regrouped(send, 2, 1, split).reshape(len(arrays), split * rows, cols)


def to_tokens(value, outs, shape, seq, group, groups, split):
    count, length, cols = value.shape
    rows = length // split
    whole = regrouped(value.reshape(count, split, rows, cols), 1, 1, split)
    results = []
    for n in range(count):
        result = jnp.zeros(shape, jnp.bfloat16) if outs is None else outs[n]
        for p in range(split):
            left = (p * groups + group) * cols
            result = lax.dynamic_update_slice(result, whole[n, p][None], (seq, 0, left))
        results.append(result)
    return results


def tie(one, other):
    return lax.optimization_barrier((one, other))


def added(one, other):
    return (one.astype(jnp.float32) + other.astype(jnp.float32)).astype(jnp.bfloat16)


def body(query, key, value, grad_out, tile_start):
    seqs, rows, _ = query.shape
    split = BLOCK // rows
    position = lax.axis_index("fsdp")
    blocks = lax.axis_size("fsdp") // split
    block = lax.axis_index("ctx") * blocks + position // split
    per_block = BLOCK // TILE
    tiles = lax.dynamic_slice_in_dim(tile_start, block * per_block, per_block, 1)
    starts = tiles * TILE - (block * BLOCK - WINDOW)
    paired = split == 2
    part = jnp.full((1,), position % 2 if paired else 0, jnp.int32)
    groups = min(HEAD_GROUPS, KV_HEADS // split)
    cols = KV_HEADS * HEAD_DIM // split // groups
    heads = cols // HEAD_DIM
    pieces = 2 if paired else 1
    chunks = [(s, h, groups) for s in range(seqs) for h in range(groups)]
    count = len(chunks)
    kv_arrays, qg_arrays = (key, value), (query, grad_out)
    straight = [paired and c == count - 1 for c in range(count)]
    kv_send, kv_came, qg_came, q_own, kv0, kv1, kv2 = ([None] * count for _ in range(7))
    dq, dq_came, d0, d1, d2, d0_came = ([None] * count for _ in range(6))
    d1_came, back, d0_more, total, total_came = ([None] * count for _ in range(5))
    outs_q, outs_kv = None, None
    token = jnp.zeros((8, 128), jnp.float32)

    def pack_kv(c):
        nonlocal token
        if not paired:
            kv0[c] = to_heads(kv_arrays, *chunks[c], split)[None]
            return
        token, results = pack(token, part, kv_arrays, *chunks[c], c == 0)
        kv_send[c] = results[0]
        if c == 0:
            kv0[c] = (results[1], results[0])

    def swap_kv(c):
        nonlocal token
        if paired:
            kv_send[c], token = tie(kv_send[c], token)
            with jax.named_scope(f"kv_swap_{c}"):
                kv_came[c] = swapped(kv_send[c])

    def wait_kv(c):
        nonlocal token
        if paired:
            kv_came[c], token = tie(kv_came[c], token)

    def swap_qg(c):
        nonlocal token
        if not paired:
            qg = to_heads(qg_arrays, *chunks[c], split)
            q_own[c] = [(qg, lambda h, *_, n=n: (n, 0, h)) for n in range(2)]
            return
        seq, group, _ = chunks[c]

        def own(h, _, y):
            return (seq, 0, (y[0] * groups + group) * heads + h)

        q_own[c] = [(a, own) for a in qg_arrays]
        token, results = pack(token, part, qg_arrays, *chunks[c], False)
        with jax.named_scope(f"qg_swap_{c}"):
            qg_came[c] = swapped(results[0])

    def wait_qg(c):
        nonlocal token
        if paired:
            qg_came[c], token = tie(qg_came[c], token)

    def hop_1(c):
        nonlocal token
        if paired and c > 0:
            token, kv0[c] = assemble(token, part, kv_arrays, kv_came[c], *chunks[c])
        with jax.named_scope(f"kv_hop_1_{c}"):
            if paired and c == 0:
                kv1[c] = [shifted(a, split, across) for across, a in enumerate(kv0[c])]
            else:
                kv1[c] = shifted(kv0[c], split)

    def hop_2(c):
        nonlocal token
        if paired and c == 0:
            token, kv1[c] = joined(token, part, kv1[c])
        else:
            kv1[c], token = tie(kv1[c], token)
        with jax.named_scope(f"kv_hop_2_{c}"):
            kv2[c] = shifted(kv1[c], split)

    def attend(c):
        nonlocal token
        if paired and c == 0:
            blocks = [[(kv0[c][0][None], 0), (kv_came[c][None], 0)]]
        else:
            blocks = [[(kv0[c], i) for i in range(pieces)]]
        blocks += [[(a, i) for i in range(pieces)] for a in (kv1[c], kv2[c])]
        came = [qg_came[c]] if paired else []
        token, *results = attention(
            token, starts[chunks[c][0]], part, q_own[c], came, blocks, cols
        )
        dq[c] = results[:-3]
        d0[c], d1[c], d2[c] = results[-3:]

    def wait_hop(c):
        nonlocal token
        kv2[c], token = tie(kv2[c], token)

    def return_1(c):
        nonlocal token
        d2[c], token = tie(d2[c], token)
        with jax.named_scope(f"back_1_{c}"):
            d1_came[c] = shifted(d2[c], -split)

    def return_2(c):
        nonlocal token
        apart = straight[c]
        token, back[c] = sums(token, part, d1[c], d1_came[c], apart)
        with jax.named_scope(f"back_2_{c}"):
            if apart:
                d0_more[c] = [shifted(a, -split, across) for across, a in enumerate(back[c])]
            else:
                d0_more[c] = shifted(back[c], -split)

    def swap_grad_kv(c):
        nonlocal token
        if straight[c]:
            send, token = tie(d0[c][1], token)
            with jax.named_scope(f"grad_kv_swap_{c}"):
                d0_came[c] = swapped(send)
        elif paired:
            token, total[c] = sums(token, part, d0[c], d0_more[c], True)
            with jax.named_scope(f"grad_kv_swap_{c}"):
                total_came[c] = swapped(total[c][1])

    def wait_grad_kv(c):
        nonlocal token
        if straight[c]:
            d0_came[c], token = tie(d0_came[c], token)

    def swap_grad_q(c):
        nonlocal token
        if paired:
            dq[c][1], token = tie(dq[c][1], token)
            with jax.named_scope(f"grad_q_swap_{c}"):
                dq_came[c] = swapped(dq[c][1])

    def put_q(c):
        nonlocal token, outs_q
        if paired:
            token, outs_q = place(
                token, part, dq[c][:1], [dq_came[c]], outs_q, query.shape, *chunks[c]
            )
        else:
            outs_q = to_tokens(dq[c][0], outs_q, query.shape, *chunks[c], split)

    def put_kv(c):
        nonlocal token, outs_kv
        if not paired:
            token, total[c] = sums(token, part, d0[c], d0_more[c], True)
            outs_kv = to_tokens(total[c][0], outs_kv, key.shape, *chunks[c], split)
            return
        if straight[c]:
            ours, theirs = [d0[c][0], d0_more[c][0]], [d0_came[c], d0_more[c][1]]
        else:
            ours, theirs = total[c][:1], [total_came[c]]
        grant = LAST_GRANT if c >= count - 2 else None
        token, outs_kv = place(token, part, ours, theirs, outs_kv, key.shape, *chunks[c], grant)

    stages = [pack_kv, swap_kv, swap_qg, hop_1, hop_2, attend, return_1, return_2]
    stages += [swap_grad_kv, swap_grad_q, put_q, put_kv]
    plan = [(stage, c) for c in range(count) for stage in stages]
    if count == 4:
        plan = [
            (pack_kv, 0), (hop_1, 0), (pack_kv, 1), (swap_kv, 1), (pack_kv, 2), (pack_kv, 3),
            (hop_1, 1), (swap_kv, 2), (swap_kv, 0), (hop_2, 0), (hop_1, 2), (swap_qg, 0),
            (wait_kv, 0), (swap_kv, 3), (hop_2, 1), (hop_1, 3), (wait_qg, 0), (swap_qg, 1),
            (hop_2, 2), (attend, 0), (hop_2, 3), (wait_qg, 1), (swap_qg, 2), (attend, 1),
            (return_1, 0), (wait_qg, 2), (swap_qg, 3), (attend, 2), (wait_hop, 3), (return_1, 1),
            (wait_qg, 3), (return_2, 0), (swap_grad_q, 0), (attend, 3), (return_1, 2), (put_q, 0),
            (swap_grad_q, 1), (return_2, 1), (return_1, 3), (swap_grad_kv, 0), (put_q, 1),
            (swap_grad_q, 2), (return_2, 2), (put_kv, 0), (put_q, 2), (swap_grad_kv, 3),
            (swap_grad_q, 3), (swap_grad_kv, 1), (put_q, 3), (wait_grad_kv, 3), (return_2, 3),
            (put_kv, 1), (swap_grad_kv, 2), (put_kv, 3), (put_kv, 2),
        ]
    for stage, c in plan:
        stage(c)
    return outs_q[0], outs_kv[0], outs_kv[1]


def solution(mesh):
    tokens = P(None, ("ctx", "fsdp"), None)
    return jax.shard_map(
        body,
        mesh=mesh,
        in_specs=(tokens, tokens, tokens, tokens, P()),
        out_specs=(tokens, tokens, tokens),
        check_vma=False,
    )
```
